32 devices in a mesh: rows: 16 (over z, y, x), cols: 2 (over core).
Axes of the slice: x: 2, y: 2, z: 4, core: 2. Of those that a mesh axis runs over, the one named last changes fastest.
Arguments:
- embeddings: bfloat16 [32768, 384], P('rows')
- test_matrix: bfloat16 [32768, 64], P('rows'), may hold values from -6 to 6
- pair_list: int32 [128, 2], P(('rows', 'cols')), may hold values from -1 to 31, as said below
Outputs:
- orthonormal_basis: float32 [32768, 64], P(('rows', 'cols'))
- upper_factor: float32 [64, 64], replicated
The draws below stay inside these ranges and needn't reach their ends.
Inputs may be any that keep to these rules, and one draw needn't show every extreme that they name: `pair_list`: device (r, c) holds 4 entries. Its live entries come first: pairs (i, j) with r * 2 <= i < (r + 1) * 2 and i <= j < min((r + 3) * 2, 32); each pair appears at most once over all devices; its other entries are -1 in both places. The device with c = 0 holds at least one live pair, the two devices of one r hold at most 4 together, and device (0, 0) holds exactly 4.
All inputs are finite; a program needn't handle non-finite values.
Results may differ from the reference program's by a relative error of at most 0.0053.
Values may be sent and summed in bfloat16 or wider, within the bound.
A program may use at most 64 MiB of HBM per device.

```python
import jax
import jax.numpy as jnp
import numpy as np
from jax import lax

E = 384
K = 64
BLK = 1024
BLK_DEV = 2
NB = 32
ROWS_ALL = 32768
PAIRS_DEV = 4


def draw_embeddings(key, part):
    rows_total = NB * BLK
    group_key, member_key, noise_key, center_key = jax.random.split(key, 4)
    row_index = jnp.arange(rows_total, dtype=jnp.int32)
    block_index = row_index // BLK
    group_shift = jax.random.randint(group_key, (rows_total,), 0, 3)
    group_index = (block_index + group_shift) // 3
    member = jax.random.randint(member_key, (rows_total,), 0, BLK)
    cluster = group_index * BLK + member

    def center_of(cluster_id):
        return jax.random.normal(jax.random.fold_in(center_key, cluster_id), (E,), jnp.float32)
    centers = jax.vmap(center_of)(cluster)
    noise = 0.35 * jax.random.normal(noise_key, (rows_total, E), jnp.float32)
    return (centers + noise).astype(jnp.bfloat16)


def draw_pair_list(key, part):
    device_rows = NB // BLK_DEV
    first_offsets = []
    second_offsets = []
    for first_local in range(BLK_DEV):
        for second_local in range(first_local, 3 * BLK_DEV):
            first_offsets.append(first_local)
            second_offsets.append(second_local)
    first_table = jnp.array(np.array(first_offsets, np.int32))
    second_table = jnp.array(np.array(second_offsets, np.int32))
    candidates = len(first_offsets)
    score_key, first_key, second_key = jax.random.split(key, 3)
    base_block = jnp.arange(device_rows, dtype=jnp.int32)[:, None] * BLK_DEV
    usable = base_block + second_table[None, :] < NB
    usable_count = jnp.sum(usable.astype(jnp.int32), axis=1)
    scores = jax.random.randint(score_key, (device_rows, candidates), 0, 2 ** 20) * 256 + jnp.arange(candidates, dtype=jnp.int32)[None, :]
    scores = jnp.where(usable, scores, scores + 2 ** 29)
    ranked = jnp.argsort(scores, axis=1)
    first_most = jnp.minimum(PAIRS_DEV, usable_count)
    first_count = jax.random.randint(first_key, (device_rows,), 1, first_most + 1)
    first_count = first_count.at[0].set(PAIRS_DEV)
    second_count = jax.random.randint(second_key, (device_rows,), 0, first_most - first_count + 1)
    slot_index = jnp.arange(PAIRS_DEV, dtype=jnp.int32)[None, :]
    first_picked = ranked[:, :PAIRS_DEV]
    second_picked = jnp.take_along_axis(ranked, jnp.minimum(first_count[:, None] + slot_index, candidates - 1), axis=1)

    def to_pairs(picked, active):
        first_ids = base_block + first_table[picked]
        second_ids = base_block + second_table[picked]
        pair_rows = jnp.stack([first_ids, second_ids], axis=-1)
        return jnp.where(active[..., None], pair_rows, -1)
    first_pairs = to_pairs(first_picked, slot_index < first_count[:, None])
    second_pairs = to_pairs(second_picked, slot_index < second_count[:, None])
    return jnp.stack([first_pairs, second_pairs], axis=1).reshape(device_rows * 2 * PAIRS_DEV, 2).astype(jnp.int32)


def level_of(stream_key, extent, cuts, least, high):
    gain = 1.0
    for axis_at, blocks in cuts:
        draws = jax.random.uniform(jax.random.fold_in(jax.random.fold_in(stream_key, 6), axis_at), (blocks,), jnp.float32, least / len(cuts), high / len(cuts))
        gain = gain * jnp.repeat(jnp.exp(draws), extent[axis_at] // blocks).reshape((-1,) + (1,) * (len(extent) - 1 - axis_at))
    return gain


def gaussian(own_key, extent, spread, reach, pieces=(), kind=jnp.bfloat16):
    result = spread * jax.random.normal(own_key, extent, jnp.float32)
    if pieces:
        result = result * level_of(own_key, extent, pieces, -0.22, 0.18)
    return jnp.clip(result, -reach, reach).astype(kind)


def setup_inputs(seed: int = 0) -> dict:
    streams_of = jax.random.split(jax.random.key(seed), 4)
    return {
        "embeddings": draw_embeddings(jax.random.fold_in(streams_of[3], 71), 0),
        "test_matrix": gaussian(streams_of[1], (ROWS_ALL, K), 1.0, 6.0, ((0, 16),)),
        "pair_list": draw_pair_list(jax.random.fold_in(streams_of[3], 71), 0),
    }


SHARPNESS = 6.0
EPSILON = 1e-06

def unit_rows(embeddings):
    widened = embeddings.astype(jnp.float32)
    inverse = lax.rsqrt(lax.optimization_barrier(jnp.sum(widened * widened, axis=1, keepdims=True)) + EPSILON)
    return (widened * inverse).astype(jnp.bfloat16)

def affinity(left_rows, right_rows):
    scores = lax.dot_general(left_rows.astype(jnp.float32), right_rows.astype(jnp.float32), (((1,), (1,)), ((), ())), preferred_element_type=jnp.float32)
    return jnp.exp(SHARPNESS * (scores - 1.0)).astype(jnp.bfloat16)

def mirror_product(affinity_tile, vectors):
    return lax.dot_general(affinity_tile.astype(jnp.float32), vectors.astype(jnp.float32), (((0,), (0,)), ((), ())), preferred_element_type=jnp.float32)

def block_at(stacked, index):
    return lax.dynamic_index_in_dim(stacked, index, 0, keepdims=False)

def apply_pairs(normed, vectors, pair_list):

    def pair_step(accumulated, entry):

        def compute(current):
            first_block = entry[0]
            second_block = entry[1]
            affinity_tile = affinity(block_at(normed, first_block), block_at(normed, second_block))
            forward = jnp.dot(affinity_tile.astype(jnp.float32), block_at(vectors, second_block).astype(jnp.float32), preferred_element_type=jnp.float32)
            backward = mirror_product(affinity_tile, block_at(vectors, first_block))
            mirror_weight = (first_block != second_block).astype(jnp.float32)
            current = current.at[first_block].add(forward)
            return current.at[second_block].add(mirror_weight * backward)
        return (lax.cond(entry[0] >= 0, compute, lambda unchanged: unchanged, accumulated), None)
    initial = jnp.zeros((normed.shape[0], normed.shape[1], vectors.shape[2]), jnp.float32)
    accumulated, _ = lax.scan(pair_step, initial, pair_list.astype(jnp.int32))
    return accumulated.reshape(-1, vectors.shape[2])

def orthonormal(sketch_rows):
    gram_matrix = lax.dot_general(sketch_rows.astype(jnp.float32), sketch_rows.astype(jnp.float32), (((0,), (0,)), ((), ())), precision=lax.Precision.HIGHEST, preferred_element_type=jnp.float32) / ROWS_ALL
    lower_factor = jnp.linalg.cholesky(gram_matrix)
    solved = lax.linalg.triangular_solve(lower_factor, sketch_rows, left_side=False, lower=True, transpose_a=True)
    return (solved, lower_factor.T)

def reference(embeddings, test_matrix, pair_list):
    normed = unit_rows(embeddings).reshape(NB, BLK, E)
    sketch_rows = apply_pairs(normed, test_matrix.reshape(NB, BLK, K), pair_list)
    panel_rows, _ = orthonormal(sketch_rows)
    image_rows = apply_pairs(normed, panel_rows.astype(jnp.bfloat16).reshape(NB, BLK, K), pair_list)
    return orthonormal(image_rows)
```

```python
import functools

import jax
import jax.numpy as jnp
from jax import lax
from jax.experimental import pallas as pl
from jax.experimental.pallas import tpu as pltpu
from jax.sharding import PartitionSpec as P

BLK = 1024
SHARPNESS = 6.0
EPSILON = 1e-06
QUAD = 4
PIECES = 4
PIECE = BLK // PIECES
TILE = 256
MESH = pl.DeviceIdType.MESH
F32 = jnp.float32
BF16 = jnp.bfloat16


def dot_nt(left, right, precision=None):
    return lax.dot_general(
        left, right, (((1,), (1,)), ((), ())), precision=precision, preferred_element_type=F32
    )


def unit_rows(rows):
    widened = rows.astype(F32)
    inverse = lax.rsqrt(jnp.sum(widened * widened, axis=1, keepdims=True) + EPSILON)
    return (widened * inverse).astype(BF16)


def factor_and_inverse(gram):
    size = gram.shape[0]
    row_at = lax.broadcasted_iota(jnp.int32, (size, size), 0)
    lane_at = lax.broadcasted_iota(jnp.int32, (size, size), 1)
    augmented = jnp.concatenate([gram, (row_at == lane_at).astype(F32)], axis=1)
    parts = [augmented[8 * t : 8 * t + 8] for t in range(size // 8)]
    within = lax.broadcasted_iota(jnp.int32, (8, 1), 0)
    done = []
    for k in range(size):
        t, s = divmod(k, 8)
        row = parts[t][s : s + 1, :]
        pivot = row[:, k : k + 1]
        done.append(row * lax.rsqrt(pivot))
        scaled = row * (1.0 / pivot)
        for u in range(t, size // 8):
            column = parts[u][:, k : k + 1]
            if u == t:
                column = jnp.where(within > s, column, 0.0)
            parts[u] = parts[u] - column * scaled
    whole = jnp.concatenate(done, axis=0)
    upper = jnp.where(row_at <= lane_at, whole[:, :size], 0.0)
    return upper, whole[:, size:]


def kernel(
    count,
    pair_ref,
    emb_ref,
    test_ref,
    basis_ref,
    upper_ref,
    win,
    vec,
    aff,
    fwd,
    mir,
    sib_out,
    sib_in,
    mir_out,
    mir_in,
    gram_out,
    gram_in,
    unit_send,
    unit_recv,
    pass_send,
    pass_recv,
    vec_send,
    vec_recv,
    sib_send,
    sib_recv,
    mir_send,
    mir_recv,
    gram_send,
    gram_recv,
):
    r = lax.axis_index("rows")
    c = lax.axis_index("cols")
    other = 1 - c
    rounds = []
    stride = QUAD
    while stride < count:
        size = min(QUAD, count // stride)
        rounds.append((stride, size))
        stride *= size

    def first_partner(d):
        at = (c * QUAD + r % QUAD + d) % (2 * QUAD)
        return at, ((r // QUAD) * QUAD + at % QUAD, at // QUAD)

    def later_partner(stride, size, d):
        at = (r // stride + d) % size
        span = stride * size
        return at, ((r // span) * span + at * stride + r % stride, c)

    def remote(src, dst, send, recv, device):
        return pltpu.make_async_remote_copy(
            src_ref=src, dst_ref=dst, send_sem=send, recv_sem=recv,
            device_id=device, device_id_type=MESH,
        )

    barrier = pltpu.get_barrier_semaphore()

    def greet(device):
        pl.semaphore_signal(barrier, inc=1, device_id=device, device_id_type=MESH)

    for d in range(1, 2 * QUAD):
        greet(first_partner(d)[1])
    for stride, size in rounds:
        for d in range(1, size):
            greet(later_partner(stride, size, d)[1])
    peers = 2 * QUAD - 1 + sum(size - 1 for _, size in rounds)
    for k in (1, 2):
        below = jnp.logical_and(r % QUAD < k, r >= k)
        above = jnp.logical_and(r % QUAD + k >= QUAD, r + k < count)
        peers = peers + below.astype(jnp.int32) + above.astype(jnp.int32)

        @pl.when(below)
        def _(k=k):
            greet((r - k, c))

        @pl.when(above)
        def _(k=k):
            greet((r + k, c))

    def normalise(block):
        for q in range(PIECES):
            rows = emb_ref[pl.ds(pl.multiple_of(block * BLK + q * PIECE, PIECE), PIECE), :]
            win[block, pl.ds(q * PIECE, PIECE), :] = unit_rows(rows)

    normalise(c)
    pl.semaphore_wait(barrier, peers)

    def piece(block, q):
        return win.at[block, pl.ds(q * PIECE, PIECE), :]

    def unit_copy(k, q, device, src_block):
        return remote(
            piece(src_block, q), piece(2 * k + c, q),
            unit_send.at[k - 1, q], unit_recv.at[k - 1, q], device,
        )

    def unit_pass(k, q):
        return remote(
            piece(2 * k + c, q), piece(2 * k + c, q),
            pass_send.at[k - 1, q], pass_recv.at[k - 1, q], (r, other),
        )

    def unit_pass_in(k, q):
        return remote(
            piece(2 * k + other, q), piece(2 * k + other, q),
            pass_send.at[k - 1, q], pass_recv.at[k - 1, q], (r, other),
        )

    even = r % 2 == 0
    for q in range(PIECES):
        @pl.when(r >= 2)
        def _(q=q):
            unit_copy(2, q, (r - 2, c), c).start()

        @pl.when(r % 2 == 1)
        def _(q=q):
            unit_copy(1, q, (r - 1, c), c).start()

    def vec_copy(p, k, device):
        return remote(
            vec.at[p, c], vec.at[p, 2 * k + c], vec_send.at[p, k], vec_recv.at[p, k], device
        )

    def vec_pass(p, k):
        return remote(
            vec.at[p, 2 * k + c], vec.at[p, 2 * k + c],
            vec_send.at[p, 2 + k if k else 0], vec_recv.at[p, 2 + k if k else 0], (r, other),
        )

    def vec_pass_in(p, k):
        return remote(
            vec.at[p, 2 * k + other], vec.at[p, 2 * k + other],
            vec_send.at[p, 2 + k if k else 0], vec_recv.at[p, 2 + k if k else 0], (r, other),
        )

    def vec_start(p):
        for k in (2, 1):
            @pl.when(r >= k)
            def _(k=k):
                vec_copy(p, k, (r - k, c)).start()

    def vec_finish(p):
        for k in (1, 2):
            @pl.when(r + k < count)
            def _(k=k):
                vec_copy(p, k, (r, other)).wait_recv()
                vec_pass(p, k).start()
        for k in (1, 2):
            @pl.when(r + k < count)
            def _(k=k):
                vec_pass_in(p, k).wait_recv()

    for b in (0, 1):
        vec[0, b] = test_ref[b * BLK : (b + 1) * BLK, :].astype(F32).T.astype(BF16)
    vec_start(0)
    normalise(other)

    for k in (1, 2):
        @pl.when(r + k >= count)
        def _(k=k):
            for b in (2 * k, 2 * k + 1):
                win[b] = jnp.zeros(win.shape[1:], BF16)
                for p in (0, 1):
                    vec[p, b] = jnp.zeros(vec.shape[2:], BF16)

        @pl.when(r < k)
        def _(k=k):
            for p in (0, 1):
                mir_in[p, k - 1] = jnp.zeros(mir_in.shape[2:], BF16)

    for q in range(PIECES):
        @pl.when(r + 2 < count)
        def _(q=q):
            unit_copy(2, q, (r, other), c).wait_recv()
            unit_pass(2, q).start()

            @pl.when(even)
            def _():
                unit_copy(1, q, (r + 1, c), 4 + c).start()

        @pl.when(r + 1 < count)
        def _(q=q):
            unit_copy(1, q, (r, other), c).wait_recv()
            unit_pass(1, q).start()
    vec_finish(0)
    for q in range(PIECES):
        for k in (1, 2):
            @pl.when(r + k < count)
            def _(k=k, q=q):
                unit_pass_in(k, q).wait_recv()

    live = jnp.int32(0)
    for slot in range(4):
        live = live + (pair_ref[slot, 0] >= 0).astype(jnp.int32)
    firsts, seconds, lives = [], [], []
    for s in (0, 1):
        rank = 2 * c + s
        entry = jnp.clip(jnp.where(rank < live, rank, 4 + rank - live), 0, 7)
        first = pair_ref[entry, 0]
        second = pair_ref[entry, 1]
        alive = first >= 0
        firsts.append(jnp.clip(first - 2 * r, 0, 1))
        seconds.append(jnp.clip(second - 2 * r, 0, 5))
        lives.append(alive)

    def multiply(p):
        for s in (0, 1):
            i, j = firsts[s], seconds[s]
            mirrored = None
            for t in range(BLK // TILE):
                span = pl.ds(t * TILE, TILE)
                if p == 0:
                    scores = dot_nt(win[i, span, :], win[j])
                    tile = jnp.exp(SHARPNESS * (scores - 1.0)).astype(BF16)
                    aff[s, span, :] = tile
                else:
                    tile = aff[s, span, :]
                fwd[s, :, span] = dot_nt(vec[p, j], tile)
                term = jnp.dot(vec[p, i, :, span], tile, preferred_element_type=F32)
                mirrored = term if mirrored is None else mirrored + term
            mir[s] = mirrored

    def weight(flag):
        return flag.astype(F32)

    def block_sum(k, side):
        total = None
        for s in (0, 1):
            here = 2 * k + side
            off = jnp.logical_and(lives[s], firsts[s] != seconds[s])
            term = weight(jnp.logical_and(off, seconds[s] == here)) * mir[s]
            if k == 0:
                term = term + weight(jnp.logical_and(lives[s], firsts[s] == here)) * fwd[s]
            total = term if total is None else total + term
        return total

    def sib_copy(p, k):
        return remote(
            sib_out.at[k], sib_in.at[p, k], sib_send.at[p, k], sib_recv.at[p, k], (r, other)
        )

    def mir_copy(p, k, device):
        return remote(
            mir_out.at[p, k - 1], mir_in.at[p, k - 1],
            mir_send.at[p, k - 1], mir_recv.at[p, k - 1], device,
        )

    def collect(p):
        for k in (2, 1, 0):
            sib_out[k] = block_sum(k, other)
            sib_copy(p, k).start()
        for k in (2, 1):
            mine = block_sum(k, c)
            sib_copy(p, k).wait_recv()
            mir_out[p, k - 1] = (mine + sib_in[p, k]).astype(BF16)

            @pl.when(r + k < count)
            def _(k=k):
                mir_copy(p, k, (r + k, c)).start()
        total = block_sum(0, c)
        sib_copy(p, 0).wait_recv()
        total = total + sib_in[p, 0]
        for k in (1, 2):
            @pl.when(r >= k)
            def _(k=k):
                mir_copy(p, k, (r, other)).wait_recv()
        for k in (1, 2):
            total = total + mir_in[p, k - 1].astype(F32)
        for k in (0, 1, 2):
            sib_copy(p, k).wait_send()
        return total

    def gram_copy(p, n, d, to, at_slot):
        return remote(
            gram_out.at[p, n], gram_in.at[p, n, at_slot],
            gram_send.at[p, n, d], gram_recv.at[p, n, at_slot], to,
        )

    def sum_over_devices(p, value):
        steps = [(2 * QUAD, first_partner, c * QUAD + r % QUAD)]
        for stride, size in rounds:
            steps.append(
                (size, functools.partial(later_partner, stride, size), (r // stride) % size)
            )
        for n, (size, partner, me) in enumerate(steps):
            gram_out[p, n] = value
            gram_in[p, n, me] = value
            for d in range(1, size):
                gram_copy(p, n, d, partner(d)[1], me).start()
            for d in range(1, size):
                at, device = partner(d)
                gram_copy(p, n, d, device, at).wait_recv()
            value = gram_in[p, n, 0]
            for m in range(1, size):
                value = value + gram_in[p, n, m]
            for d in range(1, size):
                gram_copy(p, n, d, partner(d)[1], me).wait_send()
        return value

    rows_total = count * emb_ref.shape[0]

    def orthonormal(p, total):
        gram = dot_nt(total, total, lax.Precision.HIGHEST)
        gram = sum_over_devices(p, gram) * (1.0 / rows_total)
        upper, inverse = factor_and_inverse(gram)
        solved = jnp.dot(
            inverse, total, precision=lax.Precision.HIGHEST, preferred_element_type=F32
        )
        return solved, upper

    multiply(0)
    panel, _ = orthonormal(0, collect(0))
    vec[1, c] = panel.astype(BF16)
    vec_pass(1, 0).start()
    vec_start(1)
    vec_finish(1)
    vec_pass_in(1, 0).wait_recv()
    multiply(1)
    basis, upper = orthonormal(1, collect(1))
    upper_ref[...] = upper
    basis_ref[...] = basis.T

    vec_pass(1, 0).wait_send()
    for k in (1, 2):
        @pl.when(r >= k)
        def _(k=k):
            for p in (0, 1):
                vec_copy(p, k, (r - k, c)).wait_send()

        @pl.when(r + k < count)
        def _(k=k):
            for p in (0, 1):
                vec_pass(p, k).wait_send()
                mir_copy(p, k, (r + k, c)).wait_send()
            for q in range(PIECES):
                unit_pass(k, q).wait_send()
    for q in range(PIECES):
        @pl.when(r >= 2)
        def _(q=q):
            unit_copy(2, q, (r - 2, c), c).wait_send()

        @pl.when(r % 2 == 1)
        def _(q=q):
            unit_copy(1, q, (r - 1, c), c).wait_send()

        @pl.when(jnp.logical_and(even, r + 2 < count))
        def _(q=q):
            unit_copy(1, q, (r + 1, c), 4 + c).wait_send()


def local(count, embeddings, test_matrix, pair_list):
    columns = test_matrix.shape[1]
    width = embeddings.shape[1]
    blocks = embeddings.shape[0] // BLK
    window = 3 * blocks
    group_pairs = lax.all_gather(pair_list, "cols", axis=0, tiled=True)
    steps = 1
    stride = QUAD
    while stride < count:
        stride *= min(QUAD, count // stride)
        steps += 1
    vmem = pl.BlockSpec(memory_space=pltpu.VMEM)
    dma = pltpu.SemaphoreType.DMA
    return pl.pallas_call(
        functools.partial(kernel, count),
        out_shape=(
            jax.ShapeDtypeStruct((BLK, columns), F32),
            jax.ShapeDtypeStruct((columns, columns), F32),
        ),
        in_specs=[pl.BlockSpec(memory_space=pltpu.SMEM), vmem, vmem],
        out_specs=(vmem, vmem),
        scratch_shapes=[
            pltpu.VMEM((window, BLK, width), BF16),
            pltpu.VMEM((2, window, columns, BLK), BF16),
            pltpu.VMEM((2, BLK, BLK), BF16),
            pltpu.VMEM((2, columns, BLK), F32),
            pltpu.VMEM((2, columns, BLK), F32),
            pltpu.VMEM((3, columns, BLK), F32),
            pltpu.VMEM((2, 3, columns, BLK), F32),
            pltpu.VMEM((2, 2, columns, BLK), BF16),
            pltpu.VMEM((2, 2, columns, BLK), BF16),
            pltpu.VMEM((2, steps, columns, columns), F32),
            pltpu.VMEM((2, steps, 2 * QUAD, columns, columns), F32),
            dma((2, PIECES)),
            dma((2, PIECES)),
            dma((2, PIECES)),
            dma((2, PIECES)),
            dma((2, 5)),
            dma((2, 5)),
            dma((2, 3)),
            dma((2, 3)),
            dma((2, 2)),
            dma((2, 2)),
            dma((2, steps, 2 * QUAD)),
            dma((2, steps, 2 * QUAD)),
        ],
        compiler_params=pltpu.CompilerParams(
            collective_id=0, has_side_effects=True, vmem_limit_bytes=48 * 1024 * 1024
        ),
    )(group_pairs, embeddings, test_matrix)


def solution(mesh):
    in_specs = (P("rows", None), P("rows", None), P(("rows", "cols"), None))
    out_specs = (P(("rows", "cols"), None), P())
    return jax.shard_map(
        functools.partial(local, mesh.shape["rows"]),
        mesh=mesh, in_specs=in_specs, out_specs=out_specs, check_vma=False,
    )
```

```python
import functools

import jax
import jax.numpy as jnp
from jax import lax
from jax.experimental import pallas as pl
from jax.experimental.pallas import tpu as pltpu
from jax.sharding import PartitionSpec as P

BLK = 1024
SHARPNESS = 6.0
EPSILON = 1e-06
QUAD = 4
PIECES = 4
PIECE = BLK // PIECES
SUBS = 2
SUB = PIECE // SUBS
PIVOTS = 4
MESH = pl.DeviceIdType.MESH
F32 = jnp.float32
BF16 = jnp.bfloat16


def dot_nt(left, right, precision=None):
    return lax.dot_general(
        left, right, (((1,), (1,)), ((), ())), precision=precision, preferred_element_type=F32
    )


def unit_rows(rows):
    widened = rows.astype(F32)
    inverse = lax.rsqrt(jnp.sum(widened * widened, axis=1, keepdims=True) + EPSILON)
    return (widened * inverse).astype(BF16)


def factor_and_inverse(gram):
    size = gram.shape[0]
    row_at = lax.broadcasted_iota(jnp.int32, (size, size), 0)
    lane_at = lax.broadcasted_iota(jnp.int32, (size, size), 1)
    augmented = jnp.concatenate([gram, (row_at == lane_at).astype(F32)], axis=1)
    parts = [augmented[8 * t : 8 * t + 8] for t in range(size // 8)]
    within = lax.broadcasted_iota(jnp.int32, (8, 1), 0)
    done = []
    for k in range(0, size, PIVOTS):
        t, s = divmod(k, 8)
        rows = [parts[t][s + q : s + q + 1, :] for q in range(PIVOTS)]
        columns = [
            [jnp.broadcast_to(parts[u][:, k + q : k + q + 1], (8, 2 * size)) for u in range(t, size // 8)]
            for q in range(PIVOTS)
        ]
        for q in range(PIVOTS):
            at = s + q
            pivot = columns[q][0][at : at + 1, :]
            inverse = 1.0 / pivot
            done.append(rows[q] * lax.rsqrt(pivot))
            columns[q][0] = jnp.where(within > at, columns[q][0], 0.0)
            for later in range(q + 1, PIVOTS):
                ratio = columns[later][0][at : at + 1, :] * inverse
                rows[later] = rows[later] - ratio * rows[q]
                columns[later] = [
                    mine - ratio * first for mine, first in zip(columns[later], columns[q])
                ]
            scaled = rows[q] * inverse
            for u in range(t, size // 8):
                parts[u] = parts[u] - columns[q][u - t] * scaled
    whole = jnp.concatenate(done, axis=0)
    upper = jnp.where(row_at <= lane_at, whole[:, :size], 0.0)
    return upper, whole[:, size:]


def kernel(
    count,
    pair_ref,
    emb_ref,
    test_ref,
    basis_ref,
    upper_ref,
    raw,
    own,
    win_0,
    win_1,
    win_2,
    win_3,
    vown_0,
    vown_1,
    vwin_0,
    vwin_1,
    pair_in,
    aff,
    fwd,
    mir,
    sib_out,
    sib_in,
    mir_out,
    mir_in,
    gram_out,
    gram_in,
    load_sem,
    pair_sem,
    unit_send,
    unit_recv,
    pass_send,
    pass_recv,
    vec_send,
    vec_recv,
    sib_send,
    sib_recv,
    mir_send,
    mir_recv,
    gram_send,
    gram_recv,
):
    win = (win_0, win_1, win_2, win_3)
    vown = (vown_0, vown_1)
    vwin = (vwin_0, vwin_1)
    r = lax.axis_index("rows")
    c = lax.axis_index("cols")
    other = 1 - c
    rounds = []
    stride = QUAD
    while stride < count:
        size = min(QUAD, count // stride)
        rounds.append((stride, size))
        stride *= size

    def first_partner(d):
        at = (c * QUAD + r % QUAD + d) % (2 * QUAD)
        return at, ((r // QUAD) * QUAD + at % QUAD, at // QUAD)

    def later_partner(stride, size, d):
        at = (r // stride + d) % size
        span = stride * size
        return at, ((r // span) * span + at * stride + r % stride, c)

    def remote(src, dst, send, recv, device):
        return pltpu.make_async_remote_copy(
            src_ref=src, dst_ref=dst, send_sem=send, recv_sem=recv,
            device_id=device, device_id_type=MESH,
        )

    def load(side, q):
        block = c if side == 0 else other
        span = pl.ds(pl.multiple_of(block * BLK + q * PIECE, PIECE), PIECE)
        return pltpu.make_async_copy(emb_ref.at[span, :], raw.at[span, :], load_sem.at[side, q])

    for side in (0, 1):
        for q in range(PIECES):
            load(side, q).start()

    barrier = pltpu.get_barrier_semaphore()

    def greet(device):
        pl.semaphore_signal(barrier, inc=1, device_id=device, device_id_type=MESH)

    for d in range(1, 2 * QUAD):
        greet(first_partner(d)[1])
    for stride, size in rounds:
        for d in range(1, size):
            greet(later_partner(stride, size, d)[1])
    peers = 2 * QUAD - 1 + sum(size - 1 for _, size in rounds)
    for k in (1, 2):
        below = jnp.logical_and(r % QUAD < k, r >= k)
        above = jnp.logical_and(r % QUAD + k >= QUAD, r + k < count)
        peers = peers + below.astype(jnp.int32) + above.astype(jnp.int32)

        @pl.when(below)
        def _(k=k):
            greet((r - k, c))

        @pl.when(above)
        def _(k=k):
            greet((r + k, c))

    def normalise(side, q):
        block = c if side == 0 else other
        load(side, q).wait()
        span = pl.ds(pl.multiple_of(block * BLK + q * PIECE, PIECE), PIECE)
        rows = unit_rows(raw[span, :])
        own[block, pl.ds(q * PIECE, PIECE), :] = rows
        win[q][block] = rows

    for b in (0, 1):
        block = test_ref[:, b * BLK : (b + 1) * BLK]
        vown[0][b] = block
        vwin[0][b] = block
    normalise(0, 0)
    pl.semaphore_wait(barrier, peers)

    pair_copy = remote(pair_ref, pair_in, pair_sem.at[0], pair_sem.at[1], (r, other))
    pair_copy.start()

    def piece(block, q, h):
        return win[q].at[block, pl.ds(h * SUB, SUB), :]

    def unit_copy(k, q, h, device, src_block):
        n = q * SUBS + h
        return remote(
            piece(src_block, q, h), piece(2 * k + c, q, h),
            unit_send.at[k - 1, n], unit_recv.at[k - 1, n], device,
        )

    def unit_pass(k, q, h):
        n = q * SUBS + h
        return remote(
            piece(2 * k + c, q, h), piece(2 * k + c, q, h),
            pass_send.at[k - 1, n], pass_recv.at[k - 1, n], (r, other),
        )

    def unit_pass_in(k, q, h):
        n = q * SUBS + h
        return remote(
            piece(2 * k + other, q, h), piece(2 * k + other, q, h),
            pass_send.at[k - 1, n], pass_recv.at[k - 1, n], (r, other),
        )

    even = r % 2 == 0

    def vec_copy(p, k, device):
        return remote(
            vown[p].at[c], vwin[p].at[2 * k + c], vec_send.at[p, k], vec_recv.at[p, k], device
        )

    def vec_pass(p, k):
        return remote(
            vwin[p].at[2 * k + c], vwin[p].at[2 * k + c],
            vec_send.at[p, 2 + k], vec_recv.at[p, 2 + k], (r, other),
        )

    def vec_pass_in(p, k):
        return remote(
            vwin[p].at[2 * k + other], vwin[p].at[2 * k + other],
            vec_send.at[p, 2 + k], vec_recv.at[p, 2 + k], (r, other),
        )

    def panel_copy(block):
        return remote(
            vown[1].at[block], vown[1].at[block], vec_send.at[1, 0], vec_recv.at[1, 0], (r, other)
        )

    def vec_start(p):
        for k in (2, 1):
            @pl.when(r >= k)
            def _(k=k):
                vec_copy(p, k, (r - k, c)).start()

    def vec_finish(p):
        for k in (1, 2):
            @pl.when(r + k < count)
            def _(k=k):
                vec_copy(p, k, (r, other)).wait_recv()
                vec_pass(p, k).start()
        for k in (1, 2):
            @pl.when(r + k < count)
            def _(k=k):
                vec_pass_in(p, k).wait_recv()

    vec_start(0)
    for q in range(PIECES):
        if q:
            normalise(0, q)
        for h in range(SUBS):
            @pl.when(r >= 2)
            def _(q=q, h=h):
                unit_copy(2, q, h, (r - 2, c), c).start()

            @pl.when(r % 2 == 1)
            def _(q=q, h=h):
                unit_copy(1, q, h, (r - 1, c), c).start()
    for q in range(PIECES):
        normalise(1, q)

    for k in (1, 2):
        @pl.when(r + k >= count)
        def _(k=k):
            for b in (2 * k, 2 * k + 1):
                for q in range(PIECES):
                    win[q][b] = jnp.zeros(win[q].shape[1:], BF16)
                for p in (0, 1):
                    vwin[p][b] = jnp.zeros(vwin[p].shape[1:], BF16)

        @pl.when(r < k)
        def _(k=k):
            for p in (0, 1):
                mir_in[p, k - 1] = jnp.zeros(mir_in.shape[2:], BF16)

    pair_copy.wait()
    on_first = c == 0
    live = jnp.int32(0)
    for slot in range(4):
        head = jnp.where(on_first, pair_ref[slot, 0], pair_in[slot, 0])
        live = live + (head >= 0).astype(jnp.int32)
    firsts, seconds, lives = [], [], []
    for s in (0, 1):
        rank = 2 * c + s
        in_head = rank < live
        rest = jnp.clip(rank - live, 0, 3)
        ends = []
        for side in (0, 1):
            head = jnp.where(on_first, pair_ref[rank, side], pair_in[rank, side])
            tail = jnp.where(on_first, pair_in[rest, side], pair_ref[rest, side])
            ends.append(jnp.where(in_head, head, tail))
        firsts.append(jnp.clip(ends[0] - 2 * r, 0, 1))
        seconds.append(jnp.clip(ends[1] - 2 * r, 0, 5))
        lives.append(ends[0] >= 0)

    def tile_of(s, q):
        scores = dot_nt(own[firsts[s]], win[q][seconds[s]])
        tile = jnp.exp(SHARPNESS * (scores - 1.0)).astype(BF16)
        aff[s, q] = tile
        return tile

    def mirror(p, s, q, tile):
        mir[s, :, pl.ds(q * PIECE, PIECE)] = jnp.dot(
            vown[p][firsts[s]], tile, preferred_element_type=F32
        )

    def forward(p, s, q, tile):
        return dot_nt(vwin[p][seconds[s], :, pl.ds(q * PIECE, PIECE)], tile)

    for q in range(PIECES):
        for h in range(SUBS):
            @pl.when(r + 2 < count)
            def _(q=q, h=h):
                unit_copy(2, q, h, (r, other), c).wait_recv()

                @pl.when(even)
                def _():
                    unit_copy(1, q, h, (r + 1, c), 4 + c).start()

                unit_pass(2, q, h).start()

            @pl.when(r + 1 < count)
            def _(q=q, h=h):
                unit_copy(1, q, h, (r, other), c).wait_recv()
                unit_pass(1, q, h).start()
        if q == 0:
            vec_finish(0)
        for h in range(SUBS):
            for k in (1, 2):
                @pl.when(r + k < count)
                def _(k=k, q=q, h=h):
                    unit_pass_in(k, q, h).wait_recv()
        for s in (0, 1):
            tile = tile_of(s, q)
            mirror(0, s, q, tile)
            term = forward(0, s, q, tile)
            fwd[s] = fwd[s] + term if q else term

    def weight(flag):
        return flag.astype(F32)

    def block_sum(k, side):
        total = None
        for s in (0, 1):
            here = 2 * k + side
            off = jnp.logical_and(lives[s], firsts[s] != seconds[s])
            term = weight(jnp.logical_and(off, seconds[s] == here)) * mir[s]
            if k == 0:
                term = term + weight(jnp.logical_and(lives[s], firsts[s] == here)) * fwd[s]
            total = term if total is None else total + term
        return total

    def sib_copy(p, k):
        return remote(
            sib_out.at[k], sib_in.at[p, k], sib_send.at[p, k], sib_recv.at[p, k], (r, other)
        )

    def mir_copy(p, k, device):
        return remote(
            mir_out.at[p, k - 1], mir_in.at[p, k - 1],
            mir_send.at[p, k - 1], mir_recv.at[p, k - 1], device,
        )

    def send_mirrors(p):
        for k in (2, 1):
            sib_out[k] = block_sum(k, other)
            sib_copy(p, k).start()
        for k in (2, 1):
            mine = block_sum(k, c)
            sib_copy(p, k).wait_recv()
            mir_out[p, k - 1] = (mine + sib_in[p, k]).astype(BF16)

            @pl.when(r + k < count)
            def _(k=k):
                mir_copy(p, k, (r + k, c)).start()

    def collect(p):
        sib_out[0] = block_sum(0, other)
        sib_copy(p, 0).start()
        total = block_sum(0, c)
        sib_copy(p, 0).wait_recv()
        total = total + sib_in[p, 0]
        for k in (1, 2):
            @pl.when(r >= k)
            def _(k=k):
                mir_copy(p, k, (r, other)).wait_recv()
        for k in (1, 2):
            total = total + mir_in[p, k - 1].astype(F32)
        for k in (0, 1, 2):
            sib_copy(p, k).wait_send()
        return total

    def gram_copy(p, n, d, to, at_slot):
        return remote(
            gram_out.at[p, n], gram_in.at[p, n, at_slot],
            gram_send.at[p, n, d], gram_recv.at[p, n, at_slot], to,
        )

    def sum_over_devices(p, value):
        steps = [(2 * QUAD, first_partner, c * QUAD + r % QUAD)]
        for stride, size in rounds:
            steps.append(
                (size, functools.partial(later_partner, stride, size), (r // stride) % size)
            )
        for n, (size, partner, me) in enumerate(steps):
            gram_out[p, n] = value
            gram_in[p, n, me] = value
            for d in range(1, size):
                gram_copy(p, n, d, partner(d)[1], me).start()
            for d in range(1, size):
                at, device = partner(d)
                gram_copy(p, n, d, device, at).wait_recv()
            value = gram_in[p, n, 0]
            for m in range(1, size):
                value = value + gram_in[p, n, m]
            for d in range(1, size):
                gram_copy(p, n, d, partner(d)[1], me).wait_send()
        return value

    rows_total = count * emb_ref.shape[0]

    def orthonormal(p, total):
        gram = dot_nt(total, total, lax.Precision.HIGHEST)
        gram = sum_over_devices(p, gram) * (1.0 / rows_total)
        upper, inverse = factor_and_inverse(gram)
        solved = jnp.dot(
            inverse, total, precision=lax.Precision.HIGHEST, preferred_element_type=F32
        )
        return solved, upper

    send_mirrors(0)
    panel, _ = orthonormal(0, collect(0))
    panel = panel.astype(BF16)
    vown[1][c] = panel
    panel_copy(c).start()
    vec_start(1)
    vwin[1][c] = panel
    panel_copy(other).wait_recv()
    for s in (0, 1):
        for q in range(PIECES):
            mirror(1, s, q, aff[s, q])
    send_mirrors(1)
    vwin[1][other] = vown[1][other]
    vec_finish(1)
    for s in (0, 1):
        total = forward(1, s, 0, aff[s, 0])
        for q in range(1, PIECES):
            total = total + forward(1, s, q, aff[s, q])
        fwd[s] = total
    basis, upper = orthonormal(1, collect(1))
    upper_ref[...] = upper
    basis_ref[...] = basis

    panel_copy(c).wait_send()
    for k in (1, 2):
        @pl.when(r >= k)
        def _(k=k):
            for p in (0, 1):
                vec_copy(p, k, (r - k, c)).wait_send()

        @pl.when(r + k < count)
        def _(k=k):
            for p in (0, 1):
                vec_pass(p, k).wait_send()
                mir_copy(p, k, (r + k, c)).wait_send()
            for q in range(PIECES):
                for h in range(SUBS):
                    unit_pass(k, q, h).wait_send()
    for q in range(PIECES):
        for h in range(SUBS):
            @pl.when(r >= 2)
            def _(q=q, h=h):
                unit_copy(2, q, h, (r - 2, c), c).wait_send()

            @pl.when(r % 2 == 1)
            def _(q=q, h=h):
                unit_copy(1, q, h, (r - 1, c), c).wait_send()

            @pl.when(jnp.logical_and(even, r + 2 < count))
            def _(q=q, h=h):
                unit_copy(1, q, h, (r + 1, c), 4 + c).wait_send()


def local(count, embeddings, test_matrix, pair_list):
    columns = test_matrix.shape[1]
    width = embeddings.shape[1]
    blocks = embeddings.shape[0] // BLK
    window = 3 * blocks
    steps = 1
    stride = QUAD
    while stride < count:
        stride *= min(QUAD, count // stride)
        steps += 1
    vmem = pl.BlockSpec(memory_space=pltpu.VMEM)
    dma = pltpu.SemaphoreType.DMA
    basis, upper = pl.pallas_call(
        functools.partial(kernel, count),
        out_shape=(
            jax.ShapeDtypeStruct((columns, BLK), F32),
            jax.ShapeDtypeStruct((columns, columns), F32),
        ),
        in_specs=[pl.BlockSpec(memory_space=pltpu.SMEM), pl.BlockSpec(memory_space=pl.ANY), vmem],
        out_specs=(vmem, vmem),
        scratch_shapes=[
            pltpu.VMEM((blocks * BLK, width), BF16),
            pltpu.VMEM((blocks, BLK, width), BF16),
            *[pltpu.VMEM((window, PIECE, width), BF16)] * PIECES,
            *[pltpu.VMEM((blocks, columns, BLK), BF16)] * 2,
            *[pltpu.VMEM((window, columns, BLK), BF16)] * 2,
            pltpu.SMEM(pair_list.shape, jnp.int32),
            pltpu.VMEM((2, PIECES, BLK, PIECE), BF16),
            pltpu.VMEM((2, columns, BLK), F32),
            pltpu.VMEM((2, columns, BLK), F32),
            pltpu.VMEM((3, columns, BLK), F32),
            pltpu.VMEM((2, 3, columns, BLK), F32),
            pltpu.VMEM((2, 2, columns, BLK), BF16),
            pltpu.VMEM((2, 2, columns, BLK), BF16),
            pltpu.VMEM((2, steps, columns, columns), F32),
            pltpu.VMEM((2, steps, 2 * QUAD, columns, columns), F32),
            dma((2, PIECES)),
            dma((2,)),
            dma((2, PIECES * SUBS)),
            dma((2, PIECES * SUBS)),
            dma((2, PIECES * SUBS)),
            dma((2, PIECES * SUBS)),
            dma((2, 5)),
            dma((2, 5)),
            dma((2, 3)),
            dma((2, 3)),
            dma((2, 2)),
            dma((2, 2)),
            dma((2, steps, 2 * QUAD)),
            dma((2, steps, 2 * QUAD)),
        ],
        compiler_params=pltpu.CompilerParams(
            collective_id=0, has_side_effects=True, vmem_limit_bytes=48 * 1024 * 1024
        ),
    )(pair_list, embeddings, test_matrix.T)
    return basis.T, upper


def solution(mesh):
    in_specs = (P("rows", None), P("rows", None), P(("rows", "cols"), None))
    out_specs = (P(("rows", "cols"), None), P())
    return jax.shard_map(
        functools.partial(local, mesh.shape["rows"]),
        mesh=mesh, in_specs=in_specs, out_specs=out_specs, check_vma=False,
    )
```

```python
import functools

import jax
import jax.numpy as jnp
from jax import lax
from jax.experimental import pallas as pl
from jax.experimental.pallas import tpu as pltpu
from jax.sharding import PartitionSpec as P

BLK = 1024
SHARPNESS = 6.0
EPSILON = 1e-06
QUAD = 4
PIECES = 4
PIECE = BLK // PIECES
SUBS = 2
SUB = PIECE // SUBS
PIVOTS = 4
MESH = pl.DeviceIdType.MESH
F32 = jnp.float32
BF16 = jnp.bfloat16


def dot_nt(left, right, precision=None):
    return lax.dot_general(
        left, right, (((1,), (1,)), ((), ())), precision=precision, preferred_element_type=F32
    )


def unit_rows(rows):
    widened = rows.astype(F32)
    inverse = lax.rsqrt(jnp.sum(widened * widened, axis=1, keepdims=True) + EPSILON)
    return (widened * inverse).astype(BF16)


def factor_and_inverse(gram):
    size = gram.shape[0]
    row_at = lax.broadcasted_iota(jnp.int32, (size, size), 0)
    lane_at = lax.broadcasted_iota(jnp.int32, (size, size), 1)
    augmented = jnp.concatenate([gram, (row_at == lane_at).astype(F32)], axis=1)
    parts = [augmented[8 * t : 8 * t + 8] for t in range(size // 8)]
    within = lax.broadcasted_iota(jnp.int32, (8, 1), 0)
    done = []
    for k in range(0, size, PIVOTS):
        t, s = divmod(k, 8)
        rows = [parts[t][s + q : s + q + 1, :] for q in range(PIVOTS)]
        columns = [
            [jnp.broadcast_to(parts[u][:, k + q : k + q + 1], (8, 2 * size)) for u in range(t, size // 8)]
            for q in range(PIVOTS)
        ]
        for q in range(PIVOTS):
            at = s + q
            pivot = columns[q][0][at : at + 1, :]
            inverse = 1.0 / pivot
            done.append(rows[q] * lax.rsqrt(pivot))
            columns[q][0] = jnp.where(within > at, columns[q][0], 0.0)
            for later in range(q + 1, PIVOTS):
                ratio = columns[later][0][at : at + 1, :] * inverse
                rows[later] = rows[later] - ratio * rows[q]
                columns[later] = [
                    mine - ratio * first for mine, first in zip(columns[later], columns[q])
                ]
            scaled = rows[q] * inverse
            for u in range(t, size // 8):
                parts[u] = parts[u] - columns[q][u - t] * scaled
    whole = jnp.concatenate(done, axis=0)
    upper = jnp.where(row_at <= lane_at, whole[:, :size], 0.0)
    return upper, whole[:, size:]


def kernel(
    count,
    pair_ref,
    emb_ref,
    test_ref,
    basis_ref,
    upper_ref,
    raw,
    own,
    win_0,
    win_1,
    win_2,
    win_3,
    vown_0,
    vown_1,
    vwin_0,
    vwin_1,
    pair_in,
    aff,
    fwd,
    mir,
    sib_out,
    sib_in,
    msib_out,
    msib_in,
    mir_out,
    mir_in,
    gram_out,
    gram_in,
    load_sem,
    test_sem,
    pair_sem,
    unit_send,
    unit_recv,
    pass_send,
    pass_recv,
    vec_send,
    vec_recv,
    sib_send,
    sib_recv,
    msib_send,
    msib_recv,
    mir_send,
    mir_recv,
    gram_send,
    gram_recv,
):
    win = (win_0, win_1, win_2, win_3)
    vown = (vown_0, vown_1)
    vwin = (vwin_0, vwin_1)
    r = lax.axis_index("rows")
    c = lax.axis_index("cols")
    other = 1 - c
    rounds = []
    stride = QUAD
    while stride < count:
        size = min(QUAD, count // stride)
        rounds.append((stride, size))
        stride *= size

    def first_partner(d):
        at = (c * QUAD + r % QUAD + d) % (2 * QUAD)
        return at, ((r // QUAD) * QUAD + at % QUAD, at // QUAD)

    def later_partner(stride, size, d):
        at = (r // stride + d) % size
        span = stride * size
        return at, ((r // span) * span + at * stride + r % stride, c)

    def remote(src, dst, send, recv, device):
        return pltpu.make_async_remote_copy(
            src_ref=src, dst_ref=dst, send_sem=send, recv_sem=recv,
            device_id=device, device_id_type=MESH,
        )

    def load(side, q):
        block = c if side == 0 else other
        span = pl.ds(pl.multiple_of(block * BLK + q * PIECE, PIECE), PIECE)
        return pltpu.make_async_copy(emb_ref.at[span, :], raw.at[span, :], load_sem.at[side, q])

    for side in (0, 1):
        for q in range(PIECES):
            load(side, q).start()

    def test_load(b, n, place):
        source = test_ref.at[:, pl.ds(b * BLK, BLK)]
        return pltpu.make_async_copy(source, place.at[b], test_sem.at[b, n])

    for b in (0, 1):
        for n, place in enumerate((vown_0, vwin_0)):
            test_load(b, n, place).start()

    barrier = pltpu.get_barrier_semaphore()

    def greet(device):
        pl.semaphore_signal(barrier, inc=1, device_id=device, device_id_type=MESH)

    for d in range(1, 2 * QUAD):
        greet(first_partner(d)[1])
    for stride, size in rounds:
        for d in range(1, size):
            greet(later_partner(stride, size, d)[1])
    peers = 2 * QUAD - 1 + sum(size - 1 for _, size in rounds)
    for k in (1, 2):
        below = jnp.logical_and(r % QUAD < k, r >= k)
        above = jnp.logical_and(r % QUAD + k >= QUAD, r + k < count)
        peers = peers + below.astype(jnp.int32) + above.astype(jnp.int32)

        @pl.when(below)
        def _(k=k):
            greet((r - k, c))

        @pl.when(above)
        def _(k=k):
            greet((r + k, c))

    def normalise(side, q):
        block = c if side == 0 else other
        load(side, q).wait()
        span = pl.ds(pl.multiple_of(block * BLK + q * PIECE, PIECE), PIECE)
        rows = unit_rows(raw[span, :])
        own[block, pl.ds(q * PIECE, PIECE), :] = rows
        win[q][block] = rows

    normalise(0, 0)
    for b in (0, 1):
        for n, place in enumerate((vown_0, vwin_0)):
            test_load(b, n, place).wait()
    pl.semaphore_wait(barrier, peers)

    pair_copy = remote(pair_ref, pair_in, pair_sem.at[0], pair_sem.at[1], (r, other))
    pair_copy.start()

    def piece(block, q, h):
        return win[q].at[block, pl.ds(h * SUB, SUB), :]

    def unit_copy(k, q, h, device, src_block):
        n = q * SUBS + h
        return remote(
            piece(src_block, q, h), piece(2 * k + c, q, h),
            unit_send.at[k - 1, n], unit_recv.at[k - 1, n], device,
        )

    def unit_pass(k, q, h):
        n = q * SUBS + h
        return remote(
            piece(2 * k + c, q, h), piece(2 * k + c, q, h),
            pass_send.at[k - 1, n], pass_recv.at[k - 1, n], (r, other),
        )

    def unit_pass_in(k, q, h):
        n = q * SUBS + h
        return remote(
            piece(2 * k + other, q, h), piece(2 * k + other, q, h),
            pass_send.at[k - 1, n], pass_recv.at[k - 1, n], (r, other),
        )

    even = r % 2 == 0

    def vec_copy(p, k, device):
        return remote(
            vown[p].at[c], vwin[p].at[2 * k + c], vec_send.at[p, k], vec_recv.at[p, k], device
        )

    def vec_pass(p, k):
        return remote(
            vwin[p].at[2 * k + c], vwin[p].at[2 * k + c],
            vec_send.at[p, 2 + k], vec_recv.at[p, 2 + k], (r, other),
        )

    def vec_pass_in(p, k):
        return remote(
            vwin[p].at[2 * k + other], vwin[p].at[2 * k + other],
            vec_send.at[p, 2 + k], vec_recv.at[p, 2 + k], (r, other),
        )

    def panel_copy(block):
        return remote(
            vown[1].at[block], vown[1].at[block], vec_send.at[1, 0], vec_recv.at[1, 0], (r, other)
        )

    def vec_start(p):
        for k in (2, 1):
            @pl.when(r >= k)
            def _(k=k):
                vec_copy(p, k, (r - k, c)).start()

    def vec_finish(p):
        for k in (1, 2):
            @pl.when(r + k < count)
            def _(k=k):
                vec_copy(p, k, (r, other)).wait_recv()
                vec_pass(p, k).start()
        for k in (1, 2):
            @pl.when(r + k < count)
            def _(k=k):
                vec_pass_in(p, k).wait_recv()

    vec_start(0)
    for q in range(PIECES):
        if q:
            normalise(0, q)
        for h in range(SUBS):
            @pl.when(r >= 2)
            def _(q=q, h=h):
                unit_copy(2, q, h, (r - 2, c), c).start()

            @pl.when(r % 2 == 1)
            def _(q=q, h=h):
                unit_copy(1, q, h, (r - 1, c), c).start()
    for q in range(PIECES):
        normalise(1, q)

    for k in (1, 2):
        @pl.when(r + k >= count)
        def _(k=k):
            for b in (2 * k, 2 * k + 1):
                for q in range(PIECES):
                    win[q][b] = jnp.zeros(win[q].shape[1:], BF16)
                for p in (0, 1):
                    vwin[p][b] = jnp.zeros(vwin[p].shape[1:], BF16)

        @pl.when(r < k)
        def _(k=k):
            for p in (0, 1):
                mir_in[p, k - 1] = jnp.zeros(mir_in.shape[2:], BF16)

    pair_copy.wait()
    on_first = c == 0
    live = jnp.int32(0)
    for slot in range(4):
        head = jnp.where(on_first, pair_ref[slot, 0], pair_in[slot, 0])
        live = live + (head >= 0).astype(jnp.int32)
    firsts, seconds, lives = [], [], []
    for s in (0, 1):
        rank = 2 * c + s
        in_head = rank < live
        rest = jnp.clip(rank - live, 0, 3)
        ends = []
        for side in (0, 1):
            head = jnp.where(on_first, pair_ref[rank, side], pair_in[rank, side])
            tail = jnp.where(on_first, pair_in[rest, side], pair_ref[rest, side])
            ends.append(jnp.where(in_head, head, tail))
        firsts.append(jnp.clip(ends[0] - 2 * r, 0, 1))
        seconds.append(jnp.clip(ends[1] - 2 * r, 0, 5))
        lives.append(ends[0] >= 0)

    def tile_of(s, q):
        scores = dot_nt(own[firsts[s]], win[q][seconds[s]])
        tile = jnp.exp(SHARPNESS * (scores - 1.0)).astype(BF16)
        aff[s, q] = tile
        return tile

    def mirror(p, s, q, tile):
        mir[s, :, pl.ds(q * PIECE, PIECE)] = jnp.dot(
            vown[p][firsts[s]], tile, preferred_element_type=F32
        )

    def forward(p, s, q, tile):
        return dot_nt(vwin[p][seconds[s], :, pl.ds(q * PIECE, PIECE)], tile)

    def weight(flag):
        return flag.astype(F32)

    def mirror_sum(block, span):
        total = None
        for s in (0, 1):
            off = jnp.logical_and(lives[s], firsts[s] != seconds[s])
            term = weight(jnp.logical_and(off, seconds[s] == block)) * mir[s, :, span]
            total = term if total is None else total + term
        return total

    def own_sum(block):
        total = mirror_sum(block, slice(None))
        for s in (0, 1):
            total = total + weight(jnp.logical_and(lives[s], firsts[s] == block)) * fwd[s]
        return total

    def msib_copy(p, k, q):
        return remote(
            msib_out.at[p, k - 1, q], msib_in.at[p, k - 1, q],
            msib_send.at[p, k - 1, q], msib_recv.at[p, k - 1, q], (r, other),
        )

    def mir_copy(p, k, q, device):
        return remote(
            mir_out.at[p, k - 1, q], mir_in.at[p, k - 1, q],
            mir_send.at[p, k - 1, q], mir_recv.at[p, k - 1, q], device,
        )

    def share_mirror(p, q):
        for k in (2, 1):
            msib_out[p, k - 1, q] = mirror_sum(2 * k + other, pl.ds(q * PIECE, PIECE))
            msib_copy(p, k, q).start()

    def send_mirror(p, q):
        for k in (2, 1):
            mine = mirror_sum(2 * k + c, pl.ds(q * PIECE, PIECE))
            msib_copy(p, k, q).wait_recv()
            mir_out[p, k - 1, q] = (mine + msib_in[p, k - 1, q]).astype(BF16)

            @pl.when(r + k < count)
            def _(k=k):
                mir_copy(p, k, q, (r + k, c)).start()

    def sib_copy(p):
        return remote(sib_out.at[p], sib_in.at[p], sib_send.at[p], sib_recv.at[p], (r, other))

    def collect(p):
        sib_out[p] = own_sum(other)
        sib_copy(p).start()
        total = own_sum(c)
        sib_copy(p).wait_recv()
        total = total + sib_in[p]
        for q in range(PIECES):
            for k in (1, 2):
                @pl.when(r >= k)
                def _(k=k, q=q):
                    mir_copy(p, k, q, (r, other)).wait_recv()
        parts = []
        for q in range(PIECES):
            part = total[:, q * PIECE : (q + 1) * PIECE]
            for k in (1, 2):
                part = part + mir_in[p, k - 1, q].astype(F32)
            parts.append(part)
        return jnp.concatenate(parts, axis=1)

    for q in range(PIECES):
        for h in range(SUBS):
            @pl.when(r + 2 < count)
            def _(q=q, h=h):
                unit_copy(2, q, h, (r, other), c).wait_recv()

                @pl.when(even)
                def _():
                    unit_copy(1, q, h, (r + 1, c), 4 + c).start()

                unit_pass(2, q, h).start()

            @pl.when(r + 1 < count)
            def _(q=q, h=h):
                unit_copy(1, q, h, (r, other), c).wait_recv()
                unit_pass(1, q, h).start()
        if q == 0:
            vec_finish(0)
        else:
            send_mirror(0, q - 1)
        for h in range(SUBS):
            for k in (1, 2):
                @pl.when(r + k < count)
                def _(k=k, q=q, h=h):
                    unit_pass_in(k, q, h).wait_recv()
        for s in (0, 1):
            tile = tile_of(s, q)
            mirror(0, s, q, tile)
            term = forward(0, s, q, tile)
            fwd[s] = fwd[s] + term if q else term
        share_mirror(0, q)
    send_mirror(0, PIECES - 1)

    def gram_copy(p, n, d, to, at_slot):
        return remote(
            gram_out.at[p, n], gram_in.at[p, n, at_slot],
            gram_send.at[p, n, d], gram_recv.at[p, n, at_slot], to,
        )

    def sum_over_devices(p, value):
        steps = [(2 * QUAD, first_partner, c * QUAD + r % QUAD)]
        for stride, size in rounds:
            steps.append(
                (size, functools.partial(later_partner, stride, size), (r // stride) % size)
            )
        for n, (size, partner, me) in enumerate(steps):
            gram_out[p, n] = value
            gram_in[p, n, me] = value
            for d in range(1, size):
                gram_copy(p, n, d, partner(d)[1], me).start()
            for d in range(1, size):
                at, device = partner(d)
                gram_copy(p, n, d, device, at).wait_recv()
            value = gram_in[p, n, 0]
            for m in range(1, size):
                value = value + gram_in[p, n, m]
            for d in range(1, size):
                gram_copy(p, n, d, partner(d)[1], me).wait_send()
        return value

    rows_total = count * emb_ref.shape[0]

    def orthonormal(p, total):
        gram = dot_nt(total, total, lax.Precision.HIGHEST)
        half = gram.shape[0] // 2
        packed = jnp.concatenate([gram[:half], gram[half:]], axis=1)
        packed = sum_over_devices(p, packed) * (1.0 / rows_total)
        gram = jnp.concatenate([packed[:, : 2 * half], packed[:, 2 * half :]], axis=0)
        upper, inverse = factor_and_inverse(gram)
        solved = jnp.dot(
            inverse, total, precision=lax.Precision.HIGHEST, preferred_element_type=F32
        )
        return solved, upper

    panel, _ = orthonormal(0, collect(0))
    panel = panel.astype(BF16)
    vown[1][c] = panel
    panel_copy(c).start()
    vec_start(1)
    vwin[1][c] = panel
    panel_copy(other).wait_recv()
    for q in range(PIECES):
        for s in (0, 1):
            mirror(1, s, q, aff[s, q])
        share_mirror(1, q)
        if q:
            send_mirror(1, q - 1)
    send_mirror(1, PIECES - 1)
    vwin[1][other] = vown[1][other]
    vec_finish(1)
    for s in (0, 1):
        total = forward(1, s, 0, aff[s, 0])
        for q in range(1, PIECES):
            total = total + forward(1, s, q, aff[s, q])
        fwd[s] = total
    basis, upper = orthonormal(1, collect(1))
    upper_ref[...] = upper
    basis_ref[...] = basis

    panel_copy(c).wait_send()
    for p in (0, 1):
        sib_copy(p).wait_send()
        for k in (1, 2):
            for q in range(PIECES):
                msib_copy(p, k, q).wait_send()
    for k in (1, 2):
        @pl.when(r >= k)
        def _(k=k):
            for p in (0, 1):
                vec_copy(p, k, (r - k, c)).wait_send()

        @pl.when(r + k < count)
        def _(k=k):
            for p in (0, 1):
                vec_pass(p, k).wait_send()
                for q in range(PIECES):
                    mir_copy(p, k, q, (r + k, c)).wait_send()
            for q in range(PIECES):
                for h in range(SUBS):
                    unit_pass(k, q, h).wait_send()
    for q in range(PIECES):
        for h in range(SUBS):
            @pl.when(r >= 2)
            def _(q=q, h=h):
                unit_copy(2, q, h, (r - 2, c), c).wait_send()

            @pl.when(r % 2 == 1)
            def _(q=q, h=h):
                unit_copy(1, q, h, (r - 1, c), c).wait_send()

            @pl.when(jnp.logical_and(even, r + 2 < count))
            def _(q=q, h=h):
                unit_copy(1, q, h, (r + 1, c), 4 + c).wait_send()


def local(count, embeddings, test_matrix, pair_list):
    columns = test_matrix.shape[1]
    width = embeddings.shape[1]
    blocks = embeddings.shape[0] // BLK
    window = 3 * blocks
    steps = 1
    stride = QUAD
    while stride < count:
        stride *= min(QUAD, count // stride)
        steps += 1
    vmem = pl.BlockSpec(memory_space=pltpu.VMEM)
    hbm = pl.BlockSpec(memory_space=pltpu.HBM)
    dma = pltpu.SemaphoreType.DMA
    basis, upper = pl.pallas_call(
        functools.partial(kernel, count),
        out_shape=(
            jax.ShapeDtypeStruct((columns, BLK), F32),
            jax.ShapeDtypeStruct((columns, columns), F32),
        ),
        in_specs=[pl.BlockSpec(memory_space=pltpu.SMEM), hbm, hbm],
        out_specs=(vmem, vmem),
        scratch_shapes=[
            pltpu.VMEM((blocks * BLK, width), BF16),
            pltpu.VMEM((blocks, BLK, width), BF16),
            *[pltpu.VMEM((window, PIECE, width), BF16)] * PIECES,
            *[pltpu.VMEM((blocks, columns, BLK), BF16)] * 2,
            *[pltpu.VMEM((window, columns, BLK), BF16)] * 2,
            pltpu.SMEM(pair_list.shape, jnp.int32),
            pltpu.VMEM((2, PIECES, BLK, PIECE), BF16),
            pltpu.VMEM((2, columns, BLK), F32),
            pltpu.VMEM((2, columns, BLK), F32),
            pltpu.VMEM((2, columns, BLK), F32),
            pltpu.VMEM((2, columns, BLK), F32),
            pltpu.VMEM((2, 2, PIECES, columns, PIECE), F32),
            pltpu.VMEM((2, 2, PIECES, columns, PIECE), F32),
            pltpu.VMEM((2, 2, PIECES, columns, PIECE), BF16),
            pltpu.VMEM((2, 2, PIECES, columns, PIECE), BF16),
            pltpu.VMEM((2, steps, columns // 2, 2 * columns), F32),
            pltpu.VMEM((2, steps, 2 * QUAD, columns // 2, 2 * columns), F32),
            dma((2, PIECES)),
            dma((2, 2)),
            dma((2,)),
            dma((2, PIECES * SUBS)),
            dma((2, PIECES * SUBS)),
            dma((2, PIECES * SUBS)),
            dma((2, PIECES * SUBS)),
            dma((2, 5)),
            dma((2, 5)),
            dma((2,)),
            dma((2,)),
            dma((2, 2, PIECES)),
            dma((2, 2, PIECES)),
            dma((2, 2, PIECES)),
            dma((2, 2, PIECES)),
            dma((2, steps, 2 * QUAD)),
            dma((2, steps, 2 * QUAD)),
        ],
        compiler_params=pltpu.CompilerParams(
            collective_id=0, has_side_effects=True, vmem_limit_bytes=63 * 1024 * 1024
        ),
    )(pair_list, embeddings, test_matrix.T)
    return basis.T, upper


def solution(mesh):
    in_specs = (P("rows", None), P("rows", None), P(("rows", "cols"), None))
    out_specs = (P(("rows", "cols"), None), P())
    return jax.shard_map(
        functools.partial(local, mesh.shape["rows"]),
        mesh=mesh, in_specs=in_specs, out_specs=out_specs, check_vma=False,
    )
```
